512 devices in a mesh: comp: 32 (over z, y_hi), seq: 16 (over x, y_lo, core).
Axes of the slice: x: 4, y: 8 (y_hi: 4, y_lo: 2; y = y_hi * 2 + y_lo), z: 8, core: 2. Of those that a mesh axis runs over, the one named last changes fastest.
Arguments:
- queries: bfloat16 [32, 2048, 4096], P('comp', 'seq'), may hold values from -24 to 24
- keys: bfloat16 [32, 2048, 4096], P('comp', 'seq'), may hold values from -24 to 24
- values: bfloat16 [32, 2048, 4096], P('comp', 'seq'), may hold values from -6 to 6
- latent: float32 [64, 2048], P('comp', 'seq'), may hold values from -6 to 6
- prev_denoised: float32 [64, 2048], P('comp', 'seq'), may hold values from -6 to 6
- head_weight: bfloat16 [4096, 64], P('seq'), may hold values from -0.09375 to 0.09375
Outputs:
- hidden: bfloat16 [32, 2048, 4096], P('comp', 'seq')
- new_latent: float32 [64, 2048], P('comp', 'seq')
- denoised: float32 [64, 2048], P('comp', 'seq')
The draws below stay inside these ranges and needn't reach their ends.
All inputs are finite; a program needn't handle non-finite values.
Results may differ from the reference program's by a relative error of at most 0.008.
Values may be sent and summed in bfloat16 or wider, within the bound.
No kernel may reach another device: no remote copies, remote signals or barrier semaphores. Data moves between devices by JAX's collectives and lax.ppermute only.
A program may use at most 64 MiB of HBM per device.

```python
import math
import jax
import jax.numpy as jnp
from jax import lax

HEADS = 32
HD = 128
LATENT = 64
TOKENS = 2048
COMP = 32
WIDTH = 4096


def draw_queries(key, part):
    key = jax.random.fold_in(key, 1)
    result = jnp.clip(jax.random.normal(key, (COMP, TOKENS, WIDTH), jnp.float32), -4.0, 4.0)
    return result.astype(jnp.bfloat16)


def draw_keys(key, part):
    key = jax.random.fold_in(key, 2)
    result = jnp.clip(jax.random.normal(key, (COMP, TOKENS, WIDTH), jnp.float32), -4.0, 4.0)
    return result.astype(jnp.bfloat16)


def levels(own_key, extent, shards, low, top_value):
    def one(position, parts):
        draws = jax.random.uniform(jax.random.fold_in(jax.random.fold_in(own_key, 6), position), (parts,), jnp.float32, low / len(shards), top_value / len(shards))
        return jnp.repeat(jnp.exp(draws), extent[position] // parts).reshape((-1,) + (1,) * (len(extent) - position - 1))

    factor_of = one(*shards[0])
    for cut in shards[1:]:
        factor_of = factor_of * one(*cut)
    return factor_of


def centred(own_key, extent, spread, most, split=(), dtype=jnp.bfloat16):
    drawn = jax.random.normal(own_key, extent, jnp.float32) * spread
    if len(split) > 0:
        drawn = levels(own_key, extent, split, -0.22, 0.18) * drawn
    return jnp.clip(drawn, min=-most, max=most).astype(dtype)


def setup_inputs(seed: int = 0) -> dict:
    streams_of = jax.random.split(jax.random.key(seed), 7)
    queries = draw_queries(jax.random.fold_in(streams_of[6], 71), 0)
    keys = draw_keys(jax.random.fold_in(streams_of[6], 71), 0)
    values = centred(streams_of[2], (COMP, TOKENS, WIDTH), 1.0, 6.0, ((0, 32), (1, 16)))
    latent = centred(streams_of[3], (LATENT, TOKENS), 1.0, 6.0, ((0, 32), (1, 16)), jnp.float32)
    prev_denoised = centred(streams_of[4], (LATENT, TOKENS), 1.0, 6.0, ((0, 32), (1, 16)), jnp.float32)
    head_weight = centred(streams_of[5], (WIDTH, LATENT), WIDTH ** -0.5, 0.09375, ((0, 16),))
    return {"queries": queries, "keys": keys, "values": values, "latent": latent, "prev_denoised": prev_denoised, "head_weight": head_weight}


alpha_now = 0.6
sigma_now = 0.8
alpha_next = 0.8
sigma_next = 0.6
step_before = 0.4

def head_attention(query_head, key_head, value_head):
    length = query_head.shape[0]
    block = math.gcd(length, 512)
    scale = query_head.shape[1] ** (-0.5)

    def one_block(query_block):
        scores = jnp.dot(query_block, key_head.T, preferred_element_type=jnp.float32) * scale
        highest = lax.optimization_barrier(jnp.max(scores, axis=1, keepdims=True))
        weights = jnp.exp(scores - highest)
        totals = lax.optimization_barrier(jnp.sum(weights, axis=1, keepdims=True))
        probs = (weights / totals).astype(jnp.bfloat16)
        return jnp.dot(probs, value_head, preferred_element_type=jnp.float32).astype(jnp.bfloat16)
    blocks = query_head.reshape(length // block, block, query_head.shape[1])
    return lax.map(one_block, blocks).reshape(length, query_head.shape[1])

def component_layer(operands):
    query_all, key_all, value_all = operands
    length = query_all.shape[0]

    def split_heads(array):
        return array.reshape(length, HEADS, HD).transpose(1, 0, 2)
    outputs = lax.map(lambda trio: head_attention(trio[0], trio[1], trio[2]), (split_heads(query_all), split_heads(key_all), split_heads(value_all)))
    return outputs.transpose(1, 0, 2).reshape(length, HEADS * HD)

def reference(queries, keys, values, latent, prev_denoised, head_weight):
    hidden = lax.map(component_layer, (queries, keys, values))
    last_layer = hidden[COMP - 1]
    squares = lax.optimization_barrier(jnp.mean(jnp.square(last_layer.astype(jnp.float32)), axis=1))
    norm_root = jnp.sqrt(squares + 1e-06)
    projected = jnp.dot(last_layer, head_weight, preferred_element_type=jnp.float32)
    noise = (projected / norm_root[:, None]).T
    denoised = (latent - sigma_now * noise) / alpha_now
    step_now = math.log(alpha_next / sigma_next) - math.log(alpha_now / sigma_now)
    ratio = step_before / step_now
    blend = (1.0 + 0.5 / ratio) * denoised - 0.5 / ratio * prev_denoised
    new_latent = sigma_next / sigma_now * latent - alpha_next * (math.exp(-step_now) - 1.0) * blend
    return (hidden, new_latent, denoised)
```

```python
import math

import jax
import jax.numpy as jnp
from jax import lax
from jax.experimental import pallas as pl
from jax.experimental.pallas import tpu as pltpu
from jax.sharding import PartitionSpec as P

HD = 128
BLOCK = 256

alpha_now = 0.6
sigma_now = 0.8
alpha_next = 0.8
sigma_next = 0.6
step_before = 0.4


def pack(queries, keys, values, seq_count):
    tokens, width = queries.shape
    cols = width // seq_count

    def kernel(q_ref, k_ref, v_ref, out_ref, sem):
        copies = []
        for n, ref in enumerate((q_ref, k_ref, v_ref)):
            for d in range(seq_count):
                copies.append(
                    pltpu.make_async_copy(ref.at[:, pl.ds(d * cols, cols)], out_ref.at[d, n], sem.at[n, d])
                )
        for copy in copies:
            copy.start()
        for copy in copies:
            copy.wait()

    return pl.pallas_call(
        kernel,
        out_shape=jax.ShapeDtypeStruct((seq_count, 3, tokens, cols), queries.dtype),
        in_specs=[pl.BlockSpec(memory_space=pl.ANY)] * 3,
        out_specs=pl.BlockSpec(memory_space=pl.ANY),
        scratch_shapes=[pltpu.SemaphoreType.DMA((3, seq_count))],
        name="pack",
    )(queries, keys, values)


def attention(blocks):
    seq_count, _, tokens, cols = blocks.shape
    length = seq_count * tokens
    heads = cols // HD
    group = BLOCK // tokens
    scale = HD ** (-0.5) * math.log2(math.e)

    def kernel(in_ref, out_ref, key_wide, value_wide):
        for h in range(heads):
            head = slice(h * HD, (h + 1) * HD)
            key = in_ref[:, 1, :, head].reshape(length, HD)
            key_wide[h, :, :HD] = key
            key_wide[h, :, HD:] = key
            value_wide[h, :, :HD] = in_ref[:, 2, :, head].reshape(length, HD)
            value_wide[h, :, HD:] = jnp.ones((length, HD), jnp.bfloat16)
        for h in range(heads):
            head = slice(h * HD, (h + 1) * HD)
            for b in range(0, seq_count, group):
                query = in_ref[b : b + group, 0, :, head].reshape(BLOCK, HD).astype(jnp.float32) * scale
                high = query.astype(jnp.bfloat16)
                low = (query - high.astype(jnp.float32)).astype(jnp.bfloat16)
                scores = lax.dot_general(
                    jnp.concatenate([high, low], axis=1),
                    key_wide[h],
                    (((1,), (1,)), ((), ())),
                    preferred_element_type=jnp.float32,
                )
                weights = jnp.exp2(scores - jnp.max(scores, axis=1, keepdims=True)).astype(jnp.bfloat16)
                sums = jnp.dot(weights, value_wide[h], preferred_element_type=jnp.float32)
                result = sums[:, :HD] / sums[:, HD:]
                out_ref[b : b + group, :, head] = result.astype(jnp.bfloat16).reshape(group, tokens, HD)

    return pl.pallas_call(
        kernel,
        out_shape=jax.ShapeDtypeStruct((seq_count, tokens, cols), jnp.bfloat16),
        in_specs=[pl.BlockSpec(memory_space=pltpu.VMEM)],
        out_specs=pl.BlockSpec(memory_space=pltpu.VMEM),
        scratch_shapes=[
            pltpu.VMEM((heads, length, 2 * HD), jnp.bfloat16),
            pltpu.VMEM((heads, length, 2 * HD), jnp.bfloat16),
        ],
        compiler_params=pltpu.CompilerParams(vmem_limit_bytes=56 * 1024 * 1024),
        name="attention",
    )(blocks)


def project(returned, weight, comp_count):
    seq_count, tokens, cols = returned.shape
    width, channels = weight.shape
    own = channels // comp_count

    def kernel(in_ref, weight_ref, hidden_ref, noise_ref):
        total = jnp.zeros((tokens, channels), jnp.float32)
        squares = jnp.zeros((tokens, cols), jnp.float32)
        for d in range(seq_count):
            part = in_ref[d]
            hidden_ref[:, d * cols : (d + 1) * cols] = part
            squares += jnp.square(part.astype(jnp.float32))
            total += jnp.dot(part, weight_ref[d * cols : (d + 1) * cols, :], preferred_element_type=jnp.float32)
        root = jnp.sqrt(jnp.sum(squares, axis=1, keepdims=True) / width + 1e-06)
        noise = jnp.concatenate([total / root] * (tokens // channels), axis=1).T
        noise_ref[...] = jnp.zeros(noise_ref.shape, jnp.float32)
        for c in range(comp_count):
            noise_ref[c, :own, :] = noise[c * own : (c + 1) * own, :]

    return pl.pallas_call(
        kernel,
        out_shape=(
            jax.ShapeDtypeStruct((tokens, width), jnp.bfloat16),
            jax.ShapeDtypeStruct((comp_count, 8, tokens), jnp.float32),
        ),
        in_specs=[pl.BlockSpec(memory_space=pltpu.VMEM)] * 2,
        out_specs=(pl.BlockSpec(memory_space=pltpu.VMEM),) * 2,
        compiler_params=pltpu.CompilerParams(vmem_limit_bytes=56 * 1024 * 1024),
        name="project",
    )(returned, weight)


def on_device(queries, keys, values, latent, prev_denoised, head_weight):
    seq_count = lax.axis_size("seq")
    comp_count = lax.axis_size("comp")
    own_channels = latent.shape[0]
    packed = pack(queries[0], keys[0], values[0], seq_count)
    blocks = lax.all_to_all(packed, "seq", split_axis=0, concat_axis=0, tiled=True)
    weight = lax.all_gather(head_weight, "seq", axis=0, tiled=True)
    outputs = attention(blocks)
    returned = lax.all_to_all(outputs, "seq", split_axis=0, concat_axis=0, tiled=True)
    hidden, noise = project(returned, weight, comp_count)
    everyone = lax.all_to_all(noise, "comp", split_axis=0, concat_axis=0, tiled=True)
    noise_own = everyone[comp_count - 1, :own_channels]
    denoised = (latent - sigma_now * noise_own) / alpha_now
    step_now = math.log(alpha_next / sigma_next) - math.log(alpha_now / sigma_now)
    ratio = step_before / step_now
    blend = (1.0 + 0.5 / ratio) * denoised - 0.5 / ratio * prev_denoised
    new_latent = sigma_next / sigma_now * latent - alpha_next * (math.exp(-step_now) - 1.0) * blend
    return (hidden[None], new_latent, denoised)


def solution(mesh):
    return jax.shard_map(
        on_device,
        mesh=mesh,
        in_specs=(
            P("comp", "seq", None),
            P("comp", "seq", None),
            P("comp", "seq", None),
            P("comp", "seq"),
            P("comp", "seq"),
            P("seq", None),
        ),
        out_specs=(P("comp", "seq", None), P("comp", "seq"), P("comp", "seq")),
        check_vma=False,
    )
```

```python
import math

import jax
import jax.numpy as jnp
from jax import lax
from jax.experimental import pallas as pl
from jax.experimental.pallas import tpu as pltpu
from jax.sharding import PartitionSpec as P

HD = 128
BLOCK = 256

alpha_now = 0.6
sigma_now = 0.8
alpha_next = 0.8
sigma_next = 0.6
step_before = 0.4

VMEM = pl.BlockSpec(memory_space=pltpu.VMEM)
PARAMS = pltpu.CompilerParams(vmem_limit_bytes=16 * 1024 * 1024)


def pack(queries, keys, values, seq_count):
    tokens, width = queries.shape
    cols = width // seq_count
    each = 4

    def kernel(q_ref, k_ref, v_ref, out_ref, held, in_sem, out_sem):
        incoming = [
            [
                pltpu.make_async_copy(ref.at[:, pl.ds(d * cols, cols)], held.at[d, n], in_sem.at[n, d])
                for n, ref in enumerate((q_ref, k_ref, v_ref))
            ]
            for d in range(seq_count)
        ]
        outgoing = [
            pltpu.make_async_copy(held.at[pl.ds(d, each)], out_ref.at[pl.ds(d, each)], out_sem.at[d // each])
            for d in range(0, seq_count, each)
        ]
        for copies in incoming:
            for copy in copies:
                copy.start()
        for d, copies in enumerate(incoming):
            for copy in copies:
                copy.wait()
            if d % each == each - 1:
                outgoing[d // each].start()
        for copy in outgoing:
            copy.wait()

    return pl.pallas_call(
        kernel,
        out_shape=jax.ShapeDtypeStruct((seq_count, 3, tokens, cols), queries.dtype),
        in_specs=[pl.BlockSpec(memory_space=pltpu.HBM)] * 3,
        out_specs=pl.BlockSpec(memory_space=pltpu.HBM),
        scratch_shapes=[
            pltpu.VMEM((seq_count, 3, tokens, cols), queries.dtype),
            pltpu.SemaphoreType.DMA((3, seq_count)),
            pltpu.SemaphoreType.DMA((seq_count // each,)),
        ],
        compiler_params=pltpu.CompilerParams(vmem_limit_bytes=60 * 1024 * 1024),
        name="pack",
    )(queries, keys, values)


def attention(blocks, weight):
    seq_count, _, tokens, cols = blocks.shape
    channels = weight.shape[1]
    length = seq_count * tokens
    heads = cols // HD
    group = BLOCK // tokens
    fold = cols // channels
    rows = tokens // fold

    def kernel(in_ref, weight_ref, out_ref, value_wide):
        for h in range(heads):
            value_wide[h, :, :HD] = in_ref[:, 2, :, h * HD : (h + 1) * HD].reshape(length, HD)
            value_wide[h, :, HD:] = jnp.ones((length, HD), jnp.bfloat16)
        scale = HD ** (-0.5) * math.log2(math.e)
        for h in range(heads):
            head = slice(h * HD, (h + 1) * HD)
            for b in range(0, seq_count, group):
                scores = lax.dot_general(
                    in_ref[b : b + group, 0, :, head].reshape(BLOCK, HD),
                    in_ref[:, 1, :, head].reshape(length, HD),
                    (((1,), (1,)), ((), ())),
                    preferred_element_type=jnp.float32,
                )
                highest = jnp.max(scores, axis=1, keepdims=True)
                weights = jnp.exp2((scores - highest) * scale).astype(jnp.bfloat16)
                sums = jnp.dot(weights, value_wide[h], preferred_element_type=jnp.float32)
                result = (sums[:, :HD] / sums[:, HD:]).astype(jnp.bfloat16)
                for t in range(group):
                    out_ref[b + t, :tokens, head] = result[t * tokens : (t + 1) * tokens]
        for b in range(seq_count):
            partial = jnp.dot(out_ref[b, :tokens], weight_ref[...], preferred_element_type=jnp.float32)
            partial = partial.astype(jnp.bfloat16)
            for f in range(fold):
                out_ref[b, tokens:, f * channels : (f + 1) * channels] = partial[f * rows : (f + 1) * rows]

    return pl.pallas_call(
        kernel,
        out_shape=jax.ShapeDtypeStruct((seq_count, tokens + rows, cols), jnp.bfloat16),
        in_specs=[VMEM, VMEM],
        out_specs=VMEM,
        scratch_shapes=[pltpu.VMEM((heads, length, 2 * HD), jnp.bfloat16)],
        compiler_params=pltpu.CompilerParams(vmem_limit_bytes=32 * 1024 * 1024),
        name="attention",
    )(blocks, weight)


def noise_rows(returned, tokens, comp_count):
    seq_count, total_rows, cols = returned.shape
    rows = total_rows - tokens
    channels = cols * rows // tokens
    fold = cols // channels
    own = channels // comp_count
    width = seq_count * cols

    def kernel(in_ref, noise_ref):
        squares = jnp.zeros((tokens, cols), jnp.float32)
        total = jnp.zeros((rows, cols), jnp.float32)
        for d in range(seq_count):
            squares += jnp.square(in_ref[d, :tokens].astype(jnp.float32))
            total += in_ref[d, tokens:].astype(jnp.float32)
        root = jnp.sqrt(jnp.sum(squares, axis=1, keepdims=True) / width + 1e-06)
        projected = jnp.concatenate([total[:, f * channels : (f + 1) * channels] for f in range(fold)], axis=0)
        noise = jnp.concatenate([projected / root] * (tokens // channels), axis=1).T
        noise_ref[...] = jnp.zeros(noise_ref.shape, jnp.float32)
        for c in range(comp_count):
            noise_ref[c, :own, :] = noise[c * own : (c + 1) * own, :]

    return pl.pallas_call(
        kernel,
        out_shape=jax.ShapeDtypeStruct((comp_count, 8, tokens), jnp.float32),
        in_specs=[VMEM],
        out_specs=VMEM,
        compiler_params=PARAMS,
        name="noise",
    )(returned)


def assemble(returned, tokens):
    seq_count, _, cols = returned.shape

    def kernel(in_ref, out_ref):
        for d in range(seq_count):
            out_ref[:, d * cols : (d + 1) * cols] = in_ref[d, :tokens]

    return pl.pallas_call(
        kernel,
        out_shape=jax.ShapeDtypeStruct((tokens, seq_count * cols), jnp.bfloat16),
        in_specs=[VMEM],
        out_specs=VMEM,
        compiler_params=PARAMS,
        name="assemble",
    )(returned)


def on_device(queries, keys, values, latent, prev_denoised, head_weight):
    seq_count = lax.axis_size("seq")
    comp_count = lax.axis_size("comp")
    own_channels = latent.shape[0]
    tokens = queries.shape[1]
    packed = pack(queries[0], keys[0], values[0], seq_count)
    blocks = lax.all_to_all(packed, "seq", split_axis=0, concat_axis=0, tiled=True)
    outputs = attention(blocks, head_weight)
    returned = lax.all_to_all(outputs, "seq", split_axis=0, concat_axis=0, tiled=True)
    noise = noise_rows(returned, tokens, comp_count)
    everyone = lax.all_to_all(noise, "comp", split_axis=0, concat_axis=0, tiled=True)
    hidden = assemble(returned, tokens)
    noise_own = everyone[comp_count - 1, :own_channels]
    denoised = (latent - sigma_now * noise_own) / alpha_now
    step_now = math.log(alpha_next / sigma_next) - math.log(alpha_now / sigma_now)
    ratio = step_before / step_now
    blend = (1.0 + 0.5 / ratio) * denoised - 0.5 / ratio * prev_denoised
    new_latent = sigma_next / sigma_now * latent - alpha_next * (math.exp(-step_now) - 1.0) * blend
    return (hidden[None], new_latent, denoised)


def solution(mesh):
    return jax.shard_map(
        on_device,
        mesh=mesh,
        in_specs=(
            P("comp", "seq", None),
            P("comp", "seq", None),
            P("comp", "seq", None),
            P("comp", "seq"),
            P("comp", "seq"),
            P("seq", None),
        ),
        out_specs=(P("comp", "seq", None), P("comp", "seq"), P("comp", "seq")),
        check_vma=False,
    )
```

```python
import math

import jax
import jax.numpy as jnp
from jax import lax
from jax.experimental import pallas as pl
from jax.experimental.pallas import tpu as pltpu
from jax.sharding import PartitionSpec as P

HD = 128
BLOCK = 256

alpha_now = 0.6
sigma_now = 0.8
alpha_next = 0.8
sigma_next = 0.6
step_before = 0.4

VMEM = pl.BlockSpec(memory_space=pltpu.VMEM)
PARAMS = pltpu.CompilerParams(vmem_limit_bytes=16 * 1024 * 1024)


def pack(queries, keys, values, seq_count):
    tokens, width = queries.shape
    cols = width // seq_count

    def kernel(q_ref, k_ref, v_ref, out_ref, sem):
        copies = [
            pltpu.make_async_copy(ref.at[:, pl.ds(d * cols, cols)], out_ref.at[d, n], sem.at[n, d])
            for n, ref in enumerate((q_ref, k_ref, v_ref))
            for d in range(seq_count)
        ]
        for copy in copies:
            copy.start()
        for copy in copies:
            copy.wait()

    return pl.pallas_call(
        kernel,
        out_shape=jax.ShapeDtypeStruct((seq_count, 3, tokens, cols), queries.dtype),
        in_specs=[pl.BlockSpec(memory_space=pltpu.HBM)] * 3,
        out_specs=VMEM,
        scratch_shapes=[pltpu.SemaphoreType.DMA((3, seq_count))],
        compiler_params=pltpu.CompilerParams(vmem_limit_bytes=16 * 1024 * 1024),
        name="pack",
    )(queries, keys, values)


def attention(blocks, weight):
    seq_count, _, tokens, cols = blocks.shape
    channels = weight.shape[0]
    length = seq_count * tokens
    heads = cols // HD
    group = BLOCK // tokens
    fold = cols // channels
    rows = tokens // fold

    def kernel(in_ref, weight_ref, out_ref, value_wide):
        for h in range(heads):
            value_wide[h, :, :HD] = in_ref[:, 2, :, h * HD : (h + 1) * HD].reshape(length, HD)
            value_wide[h, :, HD:] = jnp.ones((length, HD), jnp.bfloat16)
        scale = HD ** (-0.5) * math.log2(math.e)
        for h in range(heads):
            head = slice(h * HD, (h + 1) * HD)
            for b in range(0, seq_count, group):
                scores = lax.dot_general(
                    in_ref[b : b + group, 0, :, head].reshape(BLOCK, HD),
                    in_ref[:, 1, :, head].reshape(length, HD),
                    (((1,), (1,)), ((), ())),
                    preferred_element_type=jnp.float32,
                )
                highest = jnp.max(scores, axis=1, keepdims=True)
                weights = jnp.exp2((scores - highest) * scale).astype(jnp.bfloat16)
                sums = jnp.dot(weights, value_wide[h], preferred_element_type=jnp.float32)
                result = (sums[:, :HD] / sums[:, HD:]).astype(jnp.bfloat16)
                for t in range(group):
                    out_ref[b + t, :tokens, head] = result[t * tokens : (t + 1) * tokens]

        @pl.when(lax.axis_index("comp") == lax.axis_size("comp") - 1)
        def _():
            for b in range(seq_count):
                partial = lax.dot_general(
                    out_ref[b, :tokens],
                    weight_ref[...],
                    (((1,), (1,)), ((), ())),
                    preferred_element_type=jnp.float32,
                ).astype(jnp.bfloat16)
                for f in range(fold):
                    out_ref[b, tokens:, f * channels : (f + 1) * channels] = partial[f * rows : (f + 1) * rows]

    return pl.pallas_call(
        kernel,
        out_shape=jax.ShapeDtypeStruct((seq_count, tokens + rows, cols), jnp.bfloat16),
        in_specs=[VMEM, VMEM],
        out_specs=VMEM,
        scratch_shapes=[pltpu.VMEM((heads, length, 2 * HD), jnp.bfloat16)],
        compiler_params=pltpu.CompilerParams(vmem_limit_bytes=32 * 1024 * 1024),
        name="attention",
    )(blocks, weight)


def noise_rows(returned, tokens, comp_count):
    seq_count, total_rows, cols = returned.shape
    rows = total_rows - tokens
    channels = cols * rows // tokens
    fold = cols // channels
    own = channels // comp_count
    width = seq_count * cols

    def kernel(in_ref, noise_ref):
        @pl.when(lax.axis_index("comp") == comp_count - 1)
        def _():
            squares = jnp.zeros((tokens, cols), jnp.float32)
            total = jnp.zeros((rows, cols), jnp.float32)
            for d in range(seq_count):
                squares += jnp.square(in_ref[d, :tokens].astype(jnp.float32))
                total += in_ref[d, tokens:].astype(jnp.float32)
            root = jnp.sqrt(jnp.sum(squares, axis=1, keepdims=True) / width + 1e-06)
            projected = jnp.concatenate([total[:, f * channels : (f + 1) * channels] for f in range(fold)], axis=0)
            noise = jnp.concatenate([projected / root] * (tokens // channels), axis=1).T
            for c in range(comp_count):
                noise_ref[c] = noise[c * own : (c + 1) * own, :]

    return pl.pallas_call(
        kernel,
        out_shape=jax.ShapeDtypeStruct((comp_count, own, tokens), jnp.float32),
        in_specs=[VMEM],
        out_specs=VMEM,
        compiler_params=PARAMS,
        name="noise",
    )(returned)


def assemble(returned, tokens):
    seq_count, _, cols = returned.shape

    def kernel(in_ref, out_ref):
        for d in range(seq_count):
            out_ref[:, d * cols : (d + 1) * cols] = in_ref[d, :tokens]

    return pl.pallas_call(
        kernel,
        out_shape=jax.ShapeDtypeStruct((tokens, seq_count * cols), jnp.bfloat16),
        in_specs=[VMEM],
        out_specs=VMEM,
        compiler_params=PARAMS,
        name="assemble",
    )(returned)


def on_device(queries, keys, values, latent, prev_denoised, head_weight):
    seq_count = lax.axis_size("seq")
    comp_count = lax.axis_size("comp")
    tokens = queries.shape[1]
    packed = pack(*(pltpu.with_memory_space_constraint(x[0], pltpu.HBM) for x in (queries, keys, values)), seq_count)
    blocks = lax.all_to_all(packed, "seq", split_axis=0, concat_axis=0, tiled=True)
    outputs = attention(blocks, head_weight.T)
    returned = lax.all_to_all(outputs, "seq", split_axis=0, concat_axis=0, tiled=True)
    noise = noise_rows(returned, tokens, comp_count)
    everyone = lax.all_to_all(noise, "comp", split_axis=0, concat_axis=0, tiled=True)
    hidden = assemble(returned, tokens)
    noise_own = everyone[comp_count - 1]
    denoised = (latent - sigma_now * noise_own) / alpha_now
    step_now = math.log(alpha_next / sigma_next) - math.log(alpha_now / sigma_now)
    ratio = step_before / step_now
    blend = (1.0 + 0.5 / ratio) * denoised - 0.5 / ratio * prev_denoised
    new_latent = sigma_next / sigma_now * latent - alpha_next * (math.exp(-step_now) - 1.0) * blend
    return (hidden[None], new_latent, denoised)


def solution(mesh):
    return jax.shard_map(
        on_device,
        mesh=mesh,
        in_specs=(
            P("comp", "seq", None),
            P("comp", "seq", None),
            P("comp", "seq", None),
            P("comp", "seq"),
            P("comp", "seq"),
            P("seq", None),
        ),
        out_specs=(P("comp", "seq", None), P("comp", "seq"), P("comp", "seq")),
        check_vma=False,
    )
```

```python
import math

import jax
import jax.numpy as jnp
from jax import lax
from jax.experimental import pallas as pl
from jax.experimental.pallas import tpu as pltpu
from jax.sharding import PartitionSpec as P

HD = 128
BLOCK = 256
NEAR = 8

alpha_now = 0.6
sigma_now = 0.8
alpha_next = 0.8
sigma_next = 0.6
step_before = 0.4

VMEM = pl.BlockSpec(memory_space=pltpu.VMEM)
PARAMS = pltpu.CompilerParams(vmem_limit_bytes=16 * 1024 * 1024)


def pack(queries, keys, values, seq_count):
    tokens, width = queries.shape
    cols = width // seq_count
    chunks = 2
    rows = tokens // chunks

    def kernel(q_ref, k_ref, v_ref, out_ref, held, sem):
        copies = [
            [
                pltpu.make_async_copy(ref.at[pl.ds(c * rows, rows)], held.at[n, pl.ds(c * rows, rows)], sem.at[n, c])
                for c in range(chunks)
            ]
            for n, ref in enumerate((q_ref, k_ref, v_ref))
        ]
        for n in range(3):
            for copy in copies[n]:
                copy.start()
        for n in range(3):
            for c, copy in enumerate(copies[n]):
                copy.wait()
                span = slice(c * rows, (c + 1) * rows)
                for d in range(seq_count):
                    out_ref[d, n, span] = held[n, span, d * cols : (d + 1) * cols]

    return pl.pallas_call(
        kernel,
        out_shape=jax.ShapeDtypeStruct((seq_count, 3, tokens, cols), queries.dtype),
        in_specs=[pl.BlockSpec(memory_space=pltpu.HBM)] * 3,
        out_specs=VMEM,
        scratch_shapes=[
            pltpu.VMEM((3, tokens, width), queries.dtype),
            pltpu.SemaphoreType.DMA((3, chunks)),
        ],
        compiler_params=PARAMS,
        name="pack",
    )(queries, keys, values)


def attention(blocks, weight, noise_shapes=None):
    seq_count, _, tokens, cols = blocks.shape
    channels = weight.shape[0]
    length = seq_count * tokens
    heads = cols // HD
    group = BLOCK // tokens
    project = noise_shapes is None
    others = [jax.ShapeDtypeStruct((seq_count, channels + 16, tokens), jnp.bfloat16)] if project else noise_shapes

    def kernel(in_ref, weight_ref, out_ref, *other_refs):
        scale = HD ** (-0.5) * math.log2(math.e)

        def scores_of(h, b):
            head = slice(h * HD, (h + 1) * HD)
            return lax.dot_general(
                in_ref[b : b + group, 0, :, head].reshape(BLOCK, HD),
                in_ref[:, 1, :, head].reshape(length, HD),
                (((1,), (1,)), ((), ())),
                preferred_element_type=jnp.float32,
            )

        steps = [(h, b) for h in range(heads) for b in range(0, seq_count, group)]
        upcoming = scores_of(*steps[0])
        for step, (h, b) in enumerate(steps):
            scores = upcoming
            if step + 1 < len(steps):
                upcoming = scores_of(*steps[step + 1])
            head = slice(h * HD, (h + 1) * HD)
            value = in_ref[:, 2, :, head].reshape(length, HD)
            highest = jnp.max(scores, axis=1, keepdims=True)
            weights = jnp.exp2((scores - highest) * scale).astype(jnp.bfloat16)
            sums = jnp.dot(
                weights,
                jnp.concatenate([value, jnp.ones((length, HD), jnp.bfloat16)], axis=1),
                preferred_element_type=jnp.float32,
            )
            result = (sums[:, :HD] / sums[:, HD:]).astype(jnp.bfloat16)
            for t in range(group):
                out_ref[b + t, :, head] = result[t * tokens : (t + 1) * tokens]

        for part_ref in other_refs if project else ():
            contract = (((1,), (1,)), ((), ()))
            ones = jnp.ones((8, cols), jnp.bfloat16)
            for b in range(seq_count):
                hidden = out_ref[b]
                partial = lax.dot_general(weight_ref[...], hidden, contract, preferred_element_type=jnp.float32)
                part_ref[b, :channels] = partial.astype(jnp.bfloat16)
                square = jnp.square(hidden.astype(jnp.float32))
                high = square.astype(jnp.bfloat16)
                low = (square - high.astype(jnp.float32)).astype(jnp.bfloat16)
                total = lax.dot_general(ones, high, contract, preferred_element_type=jnp.float32)
                total += lax.dot_general(ones, low, contract, preferred_element_type=jnp.float32)
                coarse = total.astype(jnp.bfloat16).astype(jnp.float32)
                part_ref[b, channels:] = jnp.concatenate([coarse, total - coarse], axis=0).astype(jnp.bfloat16)

    return pl.pallas_call(
        kernel,
        out_shape=[jax.ShapeDtypeStruct((seq_count, tokens, cols), jnp.bfloat16), *others],
        in_specs=[VMEM, VMEM],
        out_specs=[VMEM] * (1 + len(others)),
        compiler_params=pltpu.CompilerParams(vmem_limit_bytes=32 * 1024 * 1024),
        name="attention",
    )(blocks, weight)


def noise_shapes_of(comp_count, own, tokens):
    run = jax.ShapeDtypeStruct((NEAR, own, tokens), jnp.float32)
    return [run] * (comp_count // NEAR) + [jax.ShapeDtypeStruct((own, tokens), jnp.float32)]


def noise_parts(returned, width, noise_shapes):
    seq_count, total_rows, tokens = returned.shape
    channels = total_rows - 16
    own = noise_shapes[-1].shape[0]

    def kernel(in_ref, *out_refs):
        total = jnp.zeros((total_rows, tokens), jnp.float32)
        for d in range(seq_count):
            total += in_ref[d].astype(jnp.float32)
        squares = total[channels : channels + 1] + total[channels + 8 : channels + 9]
        noise = total[:channels] / jnp.sqrt(squares / width + 1e-06)
        for r, out_ref in enumerate(out_refs[:-1]):
            for n in range(NEAR):
                start = (r * NEAR + n) * own
                out_ref[n] = noise[start : start + own]
        out_refs[-1][...] = noise[channels - own :]

    return pl.pallas_call(
        kernel,
        out_shape=noise_shapes,
        in_specs=[VMEM],
        out_specs=[VMEM] * len(noise_shapes),
        compiler_params=PARAMS,
        name="noise",
    )(returned)


def assemble(returned):
    seq_count, tokens, cols = returned.shape

    def kernel(in_ref, out_ref):
        for d in range(seq_count):
            out_ref[:, d * cols : (d + 1) * cols] = in_ref[d]

    return pl.pallas_call(
        kernel,
        out_shape=jax.ShapeDtypeStruct((tokens, seq_count * cols), jnp.bfloat16),
        in_specs=[VMEM],
        out_specs=VMEM,
        compiler_params=PARAMS,
        name="assemble",
    )(returned)


def on_device(queries, keys, values, latent, prev_denoised, head_weight):
    seq_count = lax.axis_size("seq")
    comp_count = lax.axis_size("comp")
    tokens = queries.shape[1]
    last = comp_count - 1
    comp = lax.axis_index("comp")
    queries, keys, values, comp = lax.optimization_barrier((queries, keys, values, comp))
    packed = pack(*(pltpu.with_memory_space_constraint(x[0], pltpu.HBM) for x in (queries, keys, values)), seq_count)
    blocks = lax.all_to_all(packed, "seq", split_axis=0, concat_axis=0, tiled=True)
    own = latent.shape[0]
    width = queries.shape[2]
    noise_shapes = noise_shapes_of(comp_count, own, tokens)
    half = NEAR // 2
    runs = [list(range(first, first + NEAR)) for first in range(0, comp_count, NEAR)]

    def exchange(array):
        return lax.all_to_all(array, "seq", split_axis=0, concat_axis=0, tiled=True)

    def exchange_grouped(array):
        group = [list(range(seq_count))]
        return lax.all_to_all(array, "seq", split_axis=0, concat_axis=0, tiled=True, axis_index_groups=group)

    def on_last(blocks, weight):
        outputs, parts = attention(blocks, weight)
        return outputs, *noise_parts(exchange(parts), width, noise_shapes)

    def elsewhere(blocks, weight):
        return tuple(attention(blocks, weight, noise_shapes))

    blocks, comp = lax.optimization_barrier((blocks, comp))
    outputs, *noise = lax.cond(comp == last, on_last, elsewhere, blocks, head_weight.T)
    sent = [lax.ppermute(noise[r], "comp", [(last, run[half - 1])]) for r, run in enumerate(runs)]
    returned = lax.cond(comp == last, exchange, exchange_grouped, outputs)
    returned, sent = lax.optimization_barrier((returned, sent))
    hidden = assemble(returned)
    part = sum(sent[1:], sent[0])

    def own_of_last(part):
        return noise[-1]

    def from_holders(part):
        holders = [(run[half - 1], run[-1] if run[-1] != last else run[-2]) for run in runs]
        passed = lax.ppermute(part[half:], "comp", holders)
        held = jnp.where(comp % NEAR == half - 1, part[:half], passed)
        result = jnp.zeros((own, tokens), jnp.float32)
        for n in range(half):
            pairs = []
            for run, (first, second) in zip(runs, holders):
                pairs += [(first, run[n]), (second, run[half + n])]
            pairs = [(source, target) for source, target in pairs if target not in (source, last)]
            if pairs:
                result += lax.ppermute(held[n], "comp", pairs)
        kept = (comp % NEAR == half - 1) | (comp % NEAR == NEAR - 1)
        result = jnp.where(kept, held[half - 1], result)
        return jnp.where(comp == last - 1, held[half - 2], result)

    noise_own = lax.cond(comp == last, own_of_last, from_holders, part)
    denoised = (latent - sigma_now * noise_own) / alpha_now
    step_now = math.log(alpha_next / sigma_next) - math.log(alpha_now / sigma_now)
    ratio = step_before / step_now
    blend = (1.0 + 0.5 / ratio) * denoised - 0.5 / ratio * prev_denoised
    new_latent = sigma_next / sigma_now * latent - alpha_next * (math.exp(-step_now) - 1.0) * blend
    return (hidden[None], new_latent, denoised)


def solution(mesh):
    return jax.shard_map(
        on_device,
        mesh=mesh,
        in_specs=(
            P("comp", "seq", None),
            P("comp", "seq", None),
            P("comp", "seq", None),
            P("comp", "seq"),
            P("comp", "seq"),
            P("seq", None),
        ),
        out_specs=(P("comp", "seq", None), P("comp", "seq"), P("comp", "seq")),
        check_vma=False,
    )
```

```python
import math

import jax
import jax.numpy as jnp
from jax import lax
from jax.experimental import pallas as pl
from jax.experimental.pallas import tpu as pltpu
from jax.sharding import PartitionSpec as P

HD = 128
BLOCK = 256
RUNS = (8, 8, 16)
ORDER = (1, 2, 0)
SENDS = (1, 2, 3)

alpha_now = 0.6
sigma_now = 0.8
alpha_next = 0.8
sigma_next = 0.6
step_before = 0.4

VMEM = pl.BlockSpec(memory_space=pltpu.VMEM)
PARAMS = pltpu.CompilerParams(vmem_limit_bytes=16 * 1024 * 1024)


def pack(queries, keys, values, seq_count):
    tokens, width = queries.shape
    cols = width // seq_count
    chunks = 2
    rows = tokens // chunks

    def kernel(q_ref, k_ref, v_ref, out_ref, held, sem):
        copies = [
            [
                pltpu.make_async_copy(ref.at[pl.ds(c * rows, rows)], held.at[n, pl.ds(c * rows, rows)], sem.at[n, c])
                for c in range(chunks)
            ]
            for n, ref in enumerate((q_ref, k_ref, v_ref))
        ]
        for n in range(3):
            for copy in copies[n]:
                copy.start()
        for n in range(3):
            for c, copy in enumerate(copies[n]):
                copy.wait()
                span = slice(c * rows, (c + 1) * rows)
                for d in range(seq_count):
                    out_ref[d, n, span] = held[n, span, d * cols : (d + 1) * cols]

    return pl.pallas_call(
        kernel,
        out_shape=jax.ShapeDtypeStruct((seq_count, 3, tokens, cols), queries.dtype),
        in_specs=[pl.BlockSpec(memory_space=pltpu.HBM)] * 3,
        out_specs=VMEM,
        scratch_shapes=[
            pltpu.VMEM((3, tokens, width), queries.dtype),
            pltpu.SemaphoreType.DMA((3, chunks)),
        ],
        compiler_params=PARAMS,
        name="pack",
    )(queries, keys, values)


def attention(blocks, weight, noise_shapes=None):
    seq_count, _, tokens, cols = blocks.shape
    channels = weight.shape[0]
    length = seq_count * tokens
    heads = cols // HD
    group = BLOCK // tokens
    project = noise_shapes is None
    others = [jax.ShapeDtypeStruct((seq_count, channels + 16, tokens), jnp.bfloat16)] if project else noise_shapes

    def kernel(in_ref, weight_ref, out_ref, *other_refs):
        scale = HD ** (-0.5) * math.log2(math.e)

        def scores_of(h, b):
            head = slice(h * HD, (h + 1) * HD)
            return lax.dot_general(
                in_ref[b : b + group, 0, :, head].reshape(BLOCK, HD),
                in_ref[:, 1, :, head].reshape(length, HD),
                (((1,), (1,)), ((), ())),
                preferred_element_type=jnp.float32,
            )

        steps = [(h, b) for h in range(heads) for b in range(0, seq_count, group)]
        upcoming = scores_of(*steps[0])
        for step, (h, b) in enumerate(steps):
            scores = upcoming
            if step + 1 < len(steps):
                upcoming = scores_of(*steps[step + 1])
            head = slice(h * HD, (h + 1) * HD)
            value = in_ref[:, 2, :, head].reshape(length, HD)
            highest = jnp.max(scores, axis=1, keepdims=True)
            weights = jnp.exp2((scores - highest) * scale).astype(jnp.bfloat16)
            sums = jnp.dot(
                weights,
                jnp.concatenate([value, jnp.ones((length, HD), jnp.bfloat16)], axis=1),
                preferred_element_type=jnp.float32,
            )
            result = (sums[:, :HD] / sums[:, HD:]).astype(jnp.bfloat16)
            for t in range(group):
                out_ref[b + t, :, head] = result[t * tokens : (t + 1) * tokens]

        for part_ref in other_refs if project else ():
            contract = (((1,), (1,)), ((), ()))
            ones = jnp.ones((8, cols), jnp.bfloat16)
            for b in range(seq_count):
                hidden = out_ref[b]
                partial = lax.dot_general(weight_ref[...], hidden, contract, preferred_element_type=jnp.float32)
                part_ref[b, :channels] = partial.astype(jnp.bfloat16)
                square = jnp.square(hidden.astype(jnp.float32))
                high = square.astype(jnp.bfloat16)
                low = (square - high.astype(jnp.float32)).astype(jnp.bfloat16)
                total = lax.dot_general(ones, high, contract, preferred_element_type=jnp.float32)
                total += lax.dot_general(ones, low, contract, preferred_element_type=jnp.float32)
                coarse = total.astype(jnp.bfloat16).astype(jnp.float32)
                part_ref[b, channels:] = jnp.concatenate([coarse, total - coarse], axis=0).astype(jnp.bfloat16)

    return pl.pallas_call(
        kernel,
        out_shape=[jax.ShapeDtypeStruct((seq_count, tokens, cols), jnp.bfloat16), *others],
        in_specs=[VMEM, VMEM],
        out_specs=[VMEM] * (1 + len(others)),
        compiler_params=pltpu.CompilerParams(vmem_limit_bytes=32 * 1024 * 1024),
        name="attention",
    )(blocks, weight)


def noise_shapes_of(own, tokens):
    runs = [jax.ShapeDtypeStruct((run, own, tokens), jnp.float32) for run in RUNS]
    return [*runs, jax.ShapeDtypeStruct((own, tokens), jnp.float32)]


def noise_parts(returned, width, noise_shapes):
    seq_count, total_rows, tokens = returned.shape
    channels = total_rows - 16
    own = noise_shapes[-1].shape[0]

    def kernel(in_ref, *out_refs):
        total = jnp.zeros((total_rows, tokens), jnp.float32)
        for d in range(seq_count):
            total += in_ref[d].astype(jnp.float32)
        squares = total[channels : channels + 1] + total[channels + 8 : channels + 9]
        noise = total[:channels] / jnp.sqrt(squares / width + 1e-06)
        start = 0
        for run, out_ref in zip(RUNS, out_refs):
            for n in range(run):
                out_ref[n] = noise[start : start + own]
                start += own
        out_refs[-1][...] = noise[channels - own :]

    return pl.pallas_call(
        kernel,
        out_shape=noise_shapes,
        in_specs=[VMEM],
        out_specs=[VMEM] * len(noise_shapes),
        compiler_params=PARAMS,
        name="noise",
    )(returned)


def assemble(returned):
    seq_count, tokens, cols = returned.shape

    def kernel(in_ref, out_ref):
        for d in range(seq_count):
            out_ref[:, d * cols : (d + 1) * cols] = in_ref[d]

    return pl.pallas_call(
        kernel,
        out_shape=jax.ShapeDtypeStruct((tokens, seq_count * cols), jnp.bfloat16),
        in_specs=[VMEM],
        out_specs=VMEM,
        compiler_params=PARAMS,
        name="assemble",
    )(returned)


def on_device(queries, keys, values, latent, prev_denoised, head_weight):
    seq_count = lax.axis_size("seq")
    comp_count = lax.axis_size("comp")
    tokens = queries.shape[1]
    last = comp_count - 1
    comp = lax.axis_index("comp")
    queries, keys, values, comp = lax.optimization_barrier((queries, keys, values, comp))
    packed = pack(*(pltpu.with_memory_space_constraint(x[0], pltpu.HBM) for x in (queries, keys, values)), seq_count)
    blocks = lax.all_to_all(packed, "seq", split_axis=0, concat_axis=0, tiled=True)
    own = latent.shape[0]
    width = queries.shape[2]
    noise_shapes = noise_shapes_of(own, tokens)
    firsts = [sum(RUNS[:r]) for r in range(len(RUNS))]

    def exchange(array):
        return lax.all_to_all(array, "seq", split_axis=0, concat_axis=0, tiled=True)

    def exchange_grouped(array):
        group = [list(range(seq_count))]
        return lax.all_to_all(array, "seq", split_axis=0, concat_axis=0, tiled=True, axis_index_groups=group)

    def on_last(blocks, weight):
        outputs, parts = attention(blocks, weight)
        return outputs, *noise_parts(exchange(parts), width, noise_shapes)

    def elsewhere(blocks, weight):
        return tuple(attention(blocks, weight, noise_shapes))

    blocks, comp = lax.optimization_barrier((blocks, comp))
    outputs, *noise = lax.cond(comp == last, on_last, elsewhere, blocks, head_weight.T)
    sent = {r: lax.ppermute(noise[r], "comp", [(last, firsts[r])]) for r in ORDER}
    returned = lax.cond(comp == last, exchange, exchange_grouped, outputs)
    hidden = assemble(returned)
    hidden, sent = lax.optimization_barrier((hidden, sent))

    def own_of_last(sent):
        return noise[-1]

    def from_holders(sent):
        pairs = [(firsts[2], firsts[2] + 8)]
        held = sent[0] + sent[1] + sent[2][:8] + lax.ppermute(sent[2][8:], "comp", pairs)
        pairs = [(c, c + 4) for c in range(0, comp_count, 8)]
        held = held[:4] + lax.ppermute(held[4:], "comp", pairs)
        result = held[0]
        for n in SENDS:
            pairs = [(c, c + n) for c in range(0, comp_count, 4) if c + n != last]
            result += lax.ppermute(held[n], "comp", pairs)
        return result

    noise_own = lax.cond(comp == last, own_of_last, from_holders, sent)
    denoised = (latent - sigma_now * noise_own) / alpha_now
    step_now = math.log(alpha_next / sigma_next) - math.log(alpha_now / sigma_now)
    ratio = step_before / step_now
    blend = (1.0 + 0.5 / ratio) * denoised - 0.5 / ratio * prev_denoised
    new_latent = sigma_next / sigma_now * latent - alpha_next * (math.exp(-step_now) - 1.0) * blend
    return (hidden[None], new_latent, denoised)


def solution(mesh):
    return jax.shard_map(
        on_device,
        mesh=mesh,
        in_specs=(
            P("comp", "seq", None),
            P("comp", "seq", None),
            P("comp", "seq", None),
            P("comp", "seq"),
            P("comp", "seq"),
            P("seq", None),
        ),
        out_specs=(P("comp", "seq", None), P("comp", "seq"), P("comp", "seq")),
        check_vma=False,
    )
```

```python
import math

import jax
import jax.numpy as jnp
from jax import lax
from jax.experimental import pallas as pl
from jax.experimental.pallas import tpu as pltpu
from jax.sharding import PartitionSpec as P

HD = 128
BLOCK = 512
RUNS = (8, 8, 16)
ORDER = (1, 2, 0)
SENDS = (1, 2, 3)

alpha_now = 0.6
sigma_now = 0.8
alpha_next = 0.8
sigma_next = 0.6
step_before = 0.4

VMEM = pl.BlockSpec(memory_space=pltpu.VMEM)
PARAMS = pltpu.CompilerParams(vmem_limit_bytes=16 * 1024 * 1024)


def pack(queries, keys, values, seq_count):
    tokens, width = queries.shape
    cols = width // seq_count
    chunks = 2
    rows = tokens // chunks

    def kernel(q_ref, k_ref, v_ref, out_ref, held, sem):
        copies = [
            [
                pltpu.make_async_copy(ref.at[pl.ds(c * rows, rows)], held.at[n, pl.ds(c * rows, rows)], sem.at[n, c])
                for c in range(chunks)
            ]
            for n, ref in enumerate((q_ref, k_ref, v_ref))
        ]
        for n in range(3):
            for copy in copies[n]:
                copy.start()
        for n in range(3):
            for c, copy in enumerate(copies[n]):
                copy.wait()
                span = slice(c * rows, (c + 1) * rows)
                for d in range(seq_count):
                    out_ref[d, n, span] = held[n, span, d * cols : (d + 1) * cols]

    return pl.pallas_call(
        kernel,
        out_shape=jax.ShapeDtypeStruct((seq_count, 3, tokens, cols), queries.dtype),
        in_specs=[pl.BlockSpec(memory_space=pltpu.HBM)] * 3,
        out_specs=VMEM,
        scratch_shapes=[
            pltpu.VMEM((3, tokens, width), queries.dtype),
            pltpu.SemaphoreType.DMA((3, chunks)),
        ],
        compiler_params=PARAMS,
        name="pack",
    )(queries, keys, values)


def attention(blocks, weight, noise_shapes=None):
    seq_count, _, tokens, cols = blocks.shape
    channels = weight.shape[0]
    length = seq_count * tokens
    heads = cols // HD
    group = BLOCK // tokens
    project = noise_shapes is None
    others = [jax.ShapeDtypeStruct((seq_count, channels + 16, tokens), jnp.bfloat16)] if project else noise_shapes

    def kernel(in_ref, weight_ref, out_ref, *other_refs):
        scale = HD ** (-0.5) * math.log2(math.e)

        def scores_of(h, b):
            head = slice(h * HD, (h + 1) * HD)
            return lax.dot_general(
                in_ref[b : b + group, 0, :, head].reshape(BLOCK, HD),
                in_ref[:, 1, :, head].reshape(length, HD),
                (((1,), (1,)), ((), ())),
                preferred_element_type=jnp.float32,
            )

        steps = [(h, b) for h in range(heads) for b in range(0, seq_count, group)]
        upcoming = scores_of(*steps[0])
        for step, (h, b) in enumerate(steps):
            scores = upcoming
            if step + 1 < len(steps):
                upcoming = scores_of(*steps[step + 1])
            head = slice(h * HD, (h + 1) * HD)
            value = in_ref[:, 2, :, head].reshape(length, HD)
            highest = jnp.max(scores, axis=1, keepdims=True)
            weights = jnp.exp2((scores - highest) * scale).astype(jnp.bfloat16)
            sums = jnp.dot(
                weights,
                jnp.concatenate([value, jnp.ones((length, HD), jnp.bfloat16)], axis=1),
                preferred_element_type=jnp.float32,
            )
            result = (sums[:, :HD] / sums[:, HD:]).astype(jnp.bfloat16)
            for t in range(group):
                out_ref[b + t, :, head] = result[t * tokens : (t + 1) * tokens]

        for part_ref in other_refs if project else ():
            contract = (((1,), (1,)), ((), ()))
            ones = jnp.ones((8, cols), jnp.bfloat16)
            for b in range(seq_count):
                hidden = out_ref[b]
                partial = lax.dot_general(weight_ref[...], hidden, contract, preferred_element_type=jnp.float32)
                part_ref[b, :channels] = partial.astype(jnp.bfloat16)
                square = jnp.square(hidden.astype(jnp.float32))
                high = square.astype(jnp.bfloat16)
                low = (square - high.astype(jnp.float32)).astype(jnp.bfloat16)
                total = lax.dot_general(ones, high, contract, preferred_element_type=jnp.float32)
                total += lax.dot_general(ones, low, contract, preferred_element_type=jnp.float32)
                coarse = total.astype(jnp.bfloat16).astype(jnp.float32)
                part_ref[b, channels:] = jnp.concatenate([coarse, total - coarse], axis=0).astype(jnp.bfloat16)

    return pl.pallas_call(
        kernel,
        out_shape=[jax.ShapeDtypeStruct((seq_count, tokens, cols), jnp.bfloat16), *others],
        in_specs=[VMEM, VMEM],
        out_specs=[VMEM] * (1 + len(others)),
        compiler_params=pltpu.CompilerParams(vmem_limit_bytes=32 * 1024 * 1024),
        name="attention",
    )(blocks, weight)


def noise_shapes_of(own, tokens):
    runs = [jax.ShapeDtypeStruct((run, own, tokens), jnp.float32) for run in RUNS]
    return [*runs, jax.ShapeDtypeStruct((own, tokens), jnp.float32)]


def noise_parts(returned, width, noise_shapes):
    seq_count, total_rows, tokens = returned.shape
    channels = total_rows - 16
    own = noise_shapes[-1].shape[0]

    def kernel(in_ref, *out_refs):
        total = jnp.zeros((total_rows, tokens), jnp.float32)
        for d in range(seq_count):
            total += in_ref[d].astype(jnp.float32)
        squares = total[channels : channels + 1] + total[channels + 8 : channels + 9]
        noise = total[:channels] / jnp.sqrt(squares / width + 1e-06)
        start = 0
        for run, out_ref in zip(RUNS, out_refs):
            for n in range(run):
                out_ref[n] = noise[start : start + own]
                start += own
        out_refs[-1][...] = noise[channels - own :]

    return pl.pallas_call(
        kernel,
        out_shape=noise_shapes,
        in_specs=[VMEM],
        out_specs=[VMEM] * len(noise_shapes),
        compiler_params=PARAMS,
        name="noise",
    )(returned)


def assemble(returned):
    seq_count, tokens, cols = returned.shape

    def kernel(in_ref, out_ref):
        for d in range(seq_count):
            out_ref[:, d * cols : (d + 1) * cols] = in_ref[d]

    return pl.pallas_call(
        kernel,
        out_shape=jax.ShapeDtypeStruct((tokens, seq_count * cols), jnp.bfloat16),
        in_specs=[VMEM],
        out_specs=VMEM,
        compiler_params=PARAMS,
        name="assemble",
    )(returned)


def on_device(queries, keys, values, latent, prev_denoised, head_weight):
    seq_count = lax.axis_size("seq")
    comp_count = lax.axis_size("comp")
    tokens = queries.shape[1]
    last = comp_count - 1
    comp = lax.axis_index("comp")
    queries, keys, values, comp = lax.optimization_barrier((queries, keys, values, comp))
    packed = pack(*(pltpu.with_memory_space_constraint(x[0], pltpu.HBM) for x in (queries, keys, values)), seq_count)
    blocks = lax.all_to_all(packed, "seq", split_axis=0, concat_axis=0, tiled=True)
    own = latent.shape[0]
    width = queries.shape[2]
    noise_shapes = noise_shapes_of(own, tokens)
    firsts = [sum(RUNS[:r]) for r in range(len(RUNS))]

    def exchange(array):
        return lax.all_to_all(array, "seq", split_axis=0, concat_axis=0, tiled=True)

    def exchange_grouped(array):
        group = [list(range(seq_count))]
        return lax.all_to_all(array, "seq", split_axis=0, concat_axis=0, tiled=True, axis_index_groups=group)

    def on_last(blocks, weight):
        outputs, parts = attention(blocks, weight)
        return outputs, *noise_parts(exchange(parts), width, noise_shapes)

    def elsewhere(blocks, weight):
        return tuple(attention(blocks, weight, noise_shapes))

    blocks, comp = lax.optimization_barrier((blocks, comp))
    outputs, *noise = lax.cond(comp == last, on_last, elsewhere, blocks, head_weight.T)
    sent = {r: lax.ppermute(noise[r], "comp", [(last, firsts[r])]) for r in ORDER}
    returned = lax.cond(comp == last, exchange, exchange_grouped, outputs)
    hidden = assemble(returned)
    hidden, sent = lax.optimization_barrier((hidden, sent))

    def own_of_last(sent):
        return noise[-1]

    def from_holders(sent):
        pairs = [(firsts[2], firsts[2] + 8)]
        held = sent[0] + sent[1] + sent[2][:8] + lax.ppermute(sent[2][8:], "comp", pairs)
        pairs = [(c, c + 4) for c in range(0, comp_count, 8)]
        held = held[:4] + lax.ppermute(held[4:], "comp", pairs)
        result = held[0]
        for n in SENDS:
            pairs = [(c, c + n) for c in range(0, comp_count, 4) if c + n != last]
            result += lax.ppermute(held[n], "comp", pairs)
        return result

    noise_own = lax.cond(comp == last, own_of_last, from_holders, sent)
    denoised = (latent - sigma_now * noise_own) / alpha_now
    step_now = math.log(alpha_next / sigma_next) - math.log(alpha_now / sigma_now)
    ratio = step_before / step_now
    blend = (1.0 + 0.5 / ratio) * denoised - 0.5 / ratio * prev_denoised
    new_latent = sigma_next / sigma_now * latent - alpha_next * (math.exp(-step_now) - 1.0) * blend
    return (hidden[None], new_latent, denoised)


def solution(mesh):
    return jax.shard_map(
        on_device,
        mesh=mesh,
        in_specs=(
            P("comp", "seq", None),
            P("comp", "seq", None),
            P("comp", "seq", None),
            P("comp", "seq"),
            P("comp", "seq"),
            P("seq", None),
        ),
        out_specs=(P("comp", "seq", None), P("comp", "seq"), P("comp", "seq")),
        check_vma=False,
    )
```
